32 devices in a mesh: groups: 2 (over x), seq: 8 (over z, y), tensor: 2 (over core).
Axes of the slice: x: 2, y: 2, z: 4, core: 2. Of those that a mesh axis runs over, the one named last changes fastest.
Arguments:
- enc_rows: bfloat16 [5120, 4096], P(('groups', 'seq')), parts along dimension 0, may hold values from -6 to 6
- enc_owner: int32 [5120], P(('groups', 'seq')), parts along dimension 0, may hold values from 0 to 7, as said below
- enc_doc: int32 [5120], P(('groups', 'seq')), parts along dimension 0, may hold values from 0 to 63, as said below
- dec_doc: int32 [4096], P(('groups', 'seq')), parts along dimension 0, may hold values from 0 to 63, as said below
- queries: bfloat16 [4096, 2048], P(('groups', 'seq'), 'tensor'), parts along dimension 0, may hold values from -120 to 120
- key_weight: bfloat16 [4096, 2048], P('seq', 'tensor'), may hold values from -0.09375 to 0.09375
- value_weight: bfloat16 [4096, 2048], P('seq', 'tensor'), may hold values from -0.09375 to 0.09375
- out_weight: bfloat16 [2048, 4096], P('tensor', 'seq'), may hold values from -0.125 to 0.125
Outputs:
- mixed: bfloat16 [4096, 4096], P(('groups', 'seq'), 'tensor'), parts along dimension 0
The draws below stay inside these ranges and needn't reach their ends.
There are 2 independent parts, one for each index of `groups`. The reference program is written for one: setup_inputs(seed, part) draws one part's arguments, and reference() takes and returns one part's arrays. A program takes and returns all parts, laid end to end along the dimension named above; an argument that names none is the same for every part. Nothing has to cross between parts.
Inputs may be any that keep to these rules, and one draw needn't show every extreme that they name: `enc_owner`: the rows of one seq device fall into aligned blocks of 80 rows, all rows of a block with one destination; the blocks of one device have different destinations, and its first block's destination is the device itself. `enc_doc`: each document's encoder rows are a run inside one such block; a block holds one or two documents. `dec_doc`: every decoder token's document has encoder rows, and all of them have the token's own seq device as destination; a document's decoder tokens stand in one run.
All inputs are finite; a program needn't handle non-finite values.
Results may differ from the reference program's by a relative error of at most 0.011.
Values may be sent and summed in bfloat16 or wider, within the bound.
A program may use at most 128 MiB of HBM per device.

```python
import math
import jax
import jax.numpy as jnp
from jax import lax

D = 4096
HEAD = 256
HEADS = 8
ENC_DEV = 320
DEC_DEV = 256
CAP = 80
BLOCKS = 4
INNER = 2048
ENC_TOTAL = 2560
N_SEQ = 8
N_TENSOR = 2


def packing_tables(key):
    base_key = jax.random.fold_in(key, 7101)
    shift_keys = jax.random.split(jax.random.fold_in(base_key, 1), N_SEQ)

    def one_source(source_key):
        shuffled = jax.random.permutation(source_key, N_SEQ - 1).astype(jnp.int32) + 1
        return jnp.concatenate([jnp.zeros((1,), jnp.int32), shuffled[:BLOCKS - 1]])
    shifts = jax.vmap(one_source)(shift_keys)
    sources = jnp.arange(N_SEQ, dtype=jnp.int32)[:, None]
    owners = (sources + shifts) % N_SEQ
    cut_points = jax.random.randint(jax.random.fold_in(base_key, 2), (N_SEQ, BLOCKS), 0, CAP).astype(jnp.int32)
    return (owners, cut_points)


def draw_enc_owner(key, part):
    owners, cut_points = packing_tables(key)
    return jnp.repeat(owners, CAP, axis=1).reshape(N_SEQ * ENC_DEV).astype(jnp.int32)


def draw_enc_doc(key, part):
    owners, cut_points = packing_tables(key)
    position = jnp.arange(CAP, dtype=jnp.int32)
    second_piece = (position[None, None, :] >= cut_points[:, :, None]).astype(jnp.int32)
    block_ids = jnp.arange(N_SEQ * BLOCKS, dtype=jnp.int32).reshape(N_SEQ, BLOCKS)
    documents = block_ids[:, :, None] * 2 + second_piece
    return documents.reshape(N_SEQ * ENC_DEV).astype(jnp.int32)


def draw_dec_doc(key, part):
    owners, cut_points = packing_tables(key)
    total_docs = N_SEQ * BLOCKS * 2
    doc_owner = jnp.repeat(owners.reshape(N_SEQ * BLOCKS), 2)
    doc_valid = jnp.stack([cut_points > 0, cut_points >= 0], axis=-1).reshape(total_docs)
    shards = jnp.arange(N_SEQ, dtype=jnp.int32)[:, None]
    doc_index = jnp.arange(total_docs, dtype=jnp.int32)[None, :]
    usable = (doc_owner[None, :] == shards) & doc_valid[None, :]
    sort_values = jnp.where(usable, doc_index, doc_index + total_docs)
    listed = jnp.sort(sort_values, axis=1)
    counts = jnp.sum(usable.astype(jnp.int32), axis=1)
    starts = jax.random.randint(jax.random.fold_in(key, 7202), (N_SEQ, DEC_DEV), 0, 2).astype(jnp.int32)
    running = jnp.cumsum(starts, axis=1).astype(jnp.int32)
    segment = running * counts[:, None] // (running[:, -1:] + 1)
    chosen = jnp.take_along_axis(listed, segment.astype(jnp.int32), axis=1)
    return chosen.reshape(N_SEQ * DEC_DEV).astype(jnp.int32)


def draw_queries(key, part):
    shape = (N_SEQ * DEC_DEV, HEADS * HEAD)
    return jnp.clip(jax.random.normal(jax.random.fold_in(key, 15), shape, jnp.float32), -6.0, 6.0).astype(jnp.bfloat16)


def block_scale(own_key, extent, pieces, least, largest):
    loudness, own = 1.0, jax.random.fold_in(own_key, 6)
    for dim, shards_of in pieces:
        draws = jnp.exp(jax.random.uniform(jax.random.fold_in(own, dim), (shards_of,), jnp.float32, least / len(pieces), largest / len(pieces)))
        loudness = loudness * jnp.repeat(draws, extent[dim] // shards_of).reshape([-1 if axis == dim else 1 for axis in range(len(extent))])
    return loudness


def bell_draw(own_key, extent, spread, limit, cuts=(), held_as=jnp.bfloat16):
    values = spread * jax.random.normal(own_key, extent, jnp.float32)
    if cuts:
        values = values * block_scale(own_key, extent, cuts, -0.22, 0.18)
    return jnp.clip(values, -limit, limit).astype(held_as)


def setup_inputs(seed: int = 0, part: int = 0) -> dict:
    key_of = jax.random.split(jax.random.key(seed), 9)
    part_keys = jax.random.split(jax.random.fold_in(key_of[8], part), 9)
    return {
        "enc_rows": bell_draw(part_keys[0], (ENC_TOTAL, D), 1.0, 6.0, ((0, 8),)),
        "enc_owner": draw_enc_owner(jax.random.fold_in(jax.random.fold_in(key_of[8], part), 71), part),
        "enc_doc": draw_enc_doc(jax.random.fold_in(jax.random.fold_in(key_of[8], part), 71), part),
        "dec_doc": draw_dec_doc(jax.random.fold_in(jax.random.fold_in(key_of[8], part), 71), part),
        "queries": draw_queries(jax.random.fold_in(jax.random.fold_in(key_of[8], part), 71), part),
        "key_weight": bell_draw(key_of[5], (D, INNER), D ** -0.5, 0.09375, ((0, 8), (1, 2))),
        "value_weight": bell_draw(key_of[6], (D, INNER), D ** -0.5, 0.09375, ((0, 8), (1, 2))),
        "out_weight": bell_draw(key_of[7], (INNER, D), INNER ** -0.5, 0.125, ((0, 2), (1, 8))),
    }


def reference(enc_rows, enc_owner, enc_doc, dec_doc, queries, key_weight, value_weight, out_weight):
    keys_all = jnp.dot(enc_rows, key_weight, preferred_element_type=jnp.float32).astype(jnp.bfloat16)
    values_all = jnp.dot(enc_rows, value_weight, preferred_element_type=jnp.float32).astype(jnp.bfloat16)
    row_index = jnp.arange(N_SEQ * ENC_DEV, dtype=jnp.int32)
    source_shard = (row_index // ENC_DEV).astype(jnp.int32)
    position = (row_index % CAP).astype(jnp.int32)
    slot_index = (source_shard * CAP + position).astype(jnp.int32)
    owner_index = enc_owner.astype(jnp.int32)
    slot_keys = jnp.zeros((N_SEQ, N_SEQ * CAP, HEADS * HEAD), jnp.bfloat16).at[owner_index, slot_index].set(keys_all)
    slot_values = jnp.zeros((N_SEQ, N_SEQ * CAP, HEADS * HEAD), jnp.bfloat16).at[owner_index, slot_index].set(values_all)
    slot_docs = jnp.full((N_SEQ, N_SEQ * CAP), -1, jnp.int32).at[owner_index, slot_index].set(enc_doc)
    query_blocks = queries.reshape(N_SEQ, DEC_DEV, HEADS, HEAD)
    doc_blocks = dec_doc.reshape(N_SEQ, DEC_DEV)
    score_scale = 1.0 / math.sqrt(HEAD)

    def attend(inputs):
        query_part, doc_part, key_part, value_part, slot_part = inputs
        key_heads = key_part.reshape(N_SEQ * CAP, HEADS, HEAD).astype(jnp.float32)
        value_heads = value_part.reshape(N_SEQ * CAP, HEADS, HEAD).astype(jnp.float32)
        scores = jnp.einsum('qhd,khd->hqk', query_part.astype(jnp.float32), key_heads) * score_scale
        matching = doc_part[:, None] == slot_part[None, :]
        scores = jnp.where(matching[None, :, :], scores, -1e+30)
        row_peak = lax.optimization_barrier(jnp.max(scores, axis=2, keepdims=True))
        exponent = jnp.exp(scores - row_peak)
        probs = (exponent / lax.optimization_barrier(jnp.sum(exponent, axis=2, keepdims=True))).astype(jnp.bfloat16)
        attended_part = jnp.einsum('hqk,khd->qhd', probs.astype(jnp.float32), value_heads)
        return attended_part.astype(jnp.bfloat16).reshape(DEC_DEV, HEADS * HEAD)
    attended = lax.map(attend, (query_blocks, doc_blocks, slot_keys, slot_values, slot_docs))
    attended = attended.reshape(N_SEQ * DEC_DEV, HEADS * HEAD)
    group_width = HEADS * HEAD // N_TENSOR
    total_sum = jnp.zeros((N_SEQ * DEC_DEV, D), jnp.float32)
    for group in range(N_TENSOR):
        columns = attended[:, group * group_width:(group + 1) * group_width]
        weight_rows = out_weight[group * group_width:(group + 1) * group_width, :]
        partial_term = jnp.dot(columns, weight_rows, preferred_element_type=jnp.float32).astype(jnp.bfloat16)
        partial_term = lax.optimization_barrier(partial_term)
        total_sum = total_sum + partial_term.astype(jnp.float32)
    return total_sum.astype(jnp.bfloat16)
```

```python
import math

import jax
import jax.numpy as jnp
from jax import lax
from jax.sharding import PartitionSpec as P

HEAD = 256


def half_columns(weight):
    width = weight.shape[1] // lax.axis_size("groups")
    return lax.dynamic_slice_in_dim(weight, lax.axis_index("groups") * width, width, axis=1)


def gather_columns(weight):
    groups = lax.axis_size("groups")
    gathered = lax.all_gather(half_columns(weight), ("groups", "seq"), axis=0, tiled=True)
    return gathered.reshape(groups, gathered.shape[0] // groups, gathered.shape[1])


def project(rows, weight):
    parts = gather_columns(weight)
    return jnp.concatenate(
        [
            jnp.dot(rows, parts[g], preferred_element_type=jnp.float32).astype(jnp.bfloat16)
            for g in range(parts.shape[0])
        ],
        axis=1,
    )


def on_device(enc_rows, enc_owner, enc_doc, dec_doc, queries, key_weight, value_weight, out_weight):
    shard_count = lax.axis_size("seq")
    me = lax.axis_index("seq")
    tensors = lax.axis_size("tensor")
    block_rows = 2 * enc_rows.shape[0] // shard_count
    block_count = enc_rows.shape[0] // block_rows
    width = enc_rows.shape[1] // tensors
    payload = lax.dynamic_slice_in_dim(enc_rows, lax.axis_index("tensor") * width, width, axis=1)
    lead = enc_owner.reshape(block_count, block_rows)[:, 0]
    targets = jnp.arange(shard_count, dtype=jnp.int32)
    blocks = payload.reshape(block_count, block_rows, width)
    packed = jnp.zeros((shard_count, block_rows, width), payload.dtype)
    for b in range(block_count):
        packed = jnp.where((lead[b] == targets)[:, None, None], blocks[b][None], packed)
    arrived = lax.all_to_all(packed, "seq", split_axis=0, concat_axis=0, tiled=True)
    arrived = lax.all_gather(
        arrived.reshape(shard_count * block_rows, width), "tensor", axis=1, tiled=True
    )
    tags = lax.all_gather(jnp.stack([enc_owner, enc_doc]), "seq", axis=0)
    tags = tags.reshape(shard_count, 2, block_count, block_rows)
    slot_docs = jnp.sum(jnp.where(tags[:, 0] == me, tags[:, 1] + 1, 0), axis=1) - 1
    slot_docs = slot_docs.reshape(shard_count * block_rows)
    keys_here = project(arrived, key_weight)
    values_here = project(arrived, value_weight)
    token_count = queries.shape[0]
    head_count = queries.shape[1] // HEAD
    query_heads = queries.reshape(token_count, head_count, HEAD)
    key_heads = keys_here.reshape(shard_count * block_rows, head_count, HEAD)
    value_heads = values_here.reshape(shard_count * block_rows, head_count, HEAD)
    score_scale = 1.0 / math.sqrt(HEAD)
    scores = (
        jnp.einsum("qhd,khd->hqk", query_heads, key_heads, preferred_element_type=jnp.float32)
        * score_scale
    )
    matching = dec_doc[:, None] == slot_docs[None, :]
    scores = jnp.where(matching[None, :, :], scores, -1e30)
    row_peak = jnp.max(scores, axis=2, keepdims=True)
    exponent = jnp.exp(scores - row_peak)
    probs = (exponent / jnp.sum(exponent, axis=2, keepdims=True)).astype(jnp.bfloat16)
    attended = jnp.einsum("hqk,khd->qhd", probs, value_heads, preferred_element_type=jnp.float32)
    attended = attended.astype(jnp.bfloat16).reshape(token_count, head_count * HEAD)
    groups = lax.axis_size("groups")
    height = out_weight.shape[0] // groups
    mine = lax.dynamic_slice_in_dim(out_weight, lax.axis_index("groups") * height, height, axis=0)
    out_parts = lax.all_gather(mine, ("groups", "seq"), axis=0, tiled=False)
    out_parts = out_parts.reshape(groups, shard_count, height, out_weight.shape[1])
    partial_rows = sum(
        jnp.einsum(
            "tk,skn->tsn",
            attended[:, g * height : (g + 1) * height],
            out_parts[g],
            preferred_element_type=jnp.float32,
        )
        for g in range(groups)
    ).reshape(token_count, shard_count * out_weight.shape[1])
    return lax.psum_scatter(
        partial_rows.astype(jnp.bfloat16), "tensor", scatter_dimension=1, tiled=True
    )


def solution(mesh):
    return jax.shard_map(
        on_device,
        mesh=mesh,
        in_specs=(
            P(("groups", "seq"), None),
            P(("groups", "seq")),
            P(("groups", "seq")),
            P(("groups", "seq")),
            P(("groups", "seq"), "tensor"),
            P("seq", "tensor"),
            P("seq", "tensor"),
            P("tensor", "seq"),
        ),
        out_specs=P(("groups", "seq"), "tensor"),
        check_vma=False,
    )
```

```python
import functools
import math

import jax
import jax.numpy as jnp
from jax import lax
from jax.experimental import pallas as pl
from jax.experimental.pallas import tpu as pltpu
from jax.sharding import PartitionSpec as P

HEAD = 256
MESH = pl.DeviceIdType.MESH


def when(condition, action):
    if condition is None:
        action()
    else:
        pl.when(condition)(action)


def exchange_kernel(
    shards, groups, tensors,
    x_ref, d_ref, k_ref, v_ref, o_ref,
    xg, dg, kg, vg, og,
    local_sem, x_send, x_recv, d_send, d_recv, t_send, t_recv,
    up_send, down_send, side_send, cross_send, recv,
):
    layers = shards // 2
    me = lax.axis_index("seq")
    group = lax.axis_index("groups")
    core = lax.axis_index("tensor")
    layer, side = me // 2, lax.rem(me, 2)
    to_group = {"groups": 1 - group}
    to_core = {"tensor": 1 - core}

    barrier = pltpu.get_barrier_semaphore()
    for j in range(1, shards):
        pl.semaphore_signal(
            barrier, inc=1, device_id={"seq": lax.rem(me + j, shards)}, device_id_type=MESH
        )
    pl.semaphore_signal(barrier, inc=1, device_id=to_group, device_id_type=MESH)
    pl.semaphore_signal(barrier, inc=1, device_id=to_core, device_id_type=MESH)
    pl.semaphore_wait(barrier, shards + 1)

    finish = []
    width = x_ref.shape[2]
    columns = pl.ds(pl.multiple_of(core * width, 128), width)

    def send(condition, make):
        when(condition, lambda: make().start())
        finish.append((condition, lambda: make().wait_send()))

    def remote(src, dst, send_sem, recv_sem, device):
        return pltpu.make_async_remote_copy(
            src_ref=src, dst_ref=dst, send_sem=send_sem, recv_sem=recv_sem,
            device_id=device, device_id_type=MESH,
        )

    for j in range(1, shards):
        target = lax.rem(me + j, shards)

        def rows_copy(target=target):
            return remote(
                x_ref.at[target], xg.at[me, :, columns],
                x_send.at[target], x_recv.at[me], {"seq": target},
            )

        def docs_copy(target=target):
            return remote(
                d_ref.at[target], dg.at[me], d_send.at[target], d_recv.at[me], {"seq": target}
            )

        send(None, rows_copy)
        send(None, docs_copy)

    weights = ((k_ref, kg, 1), (v_ref, vg, 1), (o_ref, og, 0))

    def piece_of(which, cross, owner):
        ref, axis = weights[which][0], weights[which][2]
        extent = ref.shape[axis]
        plain = extent // 4
        length = (extent - plain) // 2
        if cross:
            cut = pl.ds(pl.multiple_of(plain + owner * length, 128), length)
        else:
            cut = pl.ds(0, plain)
        return (cut, slice(None)) if axis == 0 else (slice(None), cut)

    def forward(condition, which, cross, origin, own, send_sems, device, owner):
        ref, full, _ = weights[which]
        cut = piece_of(which, cross, owner)
        number = (which * 3 + (1 + owner if cross else 0)) * shards + origin
        slot = (which * 2 + cross) * shards + origin

        def make():
            source = ref.at[cut] if own else full.at[(origin,) + cut]
            return remote(
                source, full.at[(origin,) + cut], send_sems.at[slot], recv.at[number], device
            )

        send(condition, make)

    def arrive(condition, which, cross, origin, owner):
        ref, full, _ = weights[which]
        cut = piece_of(which, cross, owner)
        number = (which * 3 + (1 + owner if cross else 0)) * shards + origin

        def wait():
            remote(
                ref.at[cut], full.at[(origin,) + cut],
                cross_send.at[0], recv.at[number], to_group,
            ).wait_recv()

        when(condition, wait)

    def both(a, b):
        return b if a is None else jnp.logical_and(a, b)

    up = {"seq": me + 2}
    down = {"seq": me - 2}
    beside = {"seq": layer * 2 + 1 - side}
    can_up = layer + 1 < layers
    can_down = layer >= 1

    for which in range(3):
        for cross in (0, 1):
            forward(can_up, which, cross, me, True, up_send, up, group)
            forward(can_down, which, cross, me, True, down_send, down, group)
            forward(None, which, cross, me, True, side_send, beside, group)

    own_copies = [
        pltpu.make_async_copy(x_ref.at[me], xg.at[me, :, columns], local_sem.at[0]),
        pltpu.make_async_copy(d_ref.at[me], dg.at[me], local_sem.at[1]),
        pltpu.make_async_copy(k_ref, kg.at[me], local_sem.at[2]),
        pltpu.make_async_copy(v_ref, vg.at[me], local_sem.at[3]),
        pltpu.make_async_copy(o_ref, og.at[me], local_sem.at[4]),
    ]
    for copy in own_copies:
        copy.start()

    def own_rows():
        return remote(
            x_ref.at[me], xg.at[me, :, columns], t_send.at[me], t_recv.at[me], to_core
        )

    send(None, own_rows)

    def along(distance):
        for which in range(3):
            for cross in (0, 1):
                for sign in (-1, 1):
                    there = layer + sign * distance
                    origin = there * 2 + side
                    exists = there >= 0 if sign < 0 else there < layers
                    arrive(exists, which, cross, origin, group)
                    if sign < 0:
                        forward(
                            both(exists, can_up), which, cross, origin, False, up_send, up, group
                        )
                    else:
                        forward(
                            both(exists, can_down), which, cross, origin, False,
                            down_send, down, group,
                        )
                    forward(exists, which, cross, origin, False, side_send, beside, group)
                    if cross:
                        forward(exists, which, 1, origin, False, cross_send, to_group, group)

    def across(distance):
        for which in range(3):
            for cross in (0, 1):
                for sign in (-1, 1) if distance else (1,):
                    there = layer + sign * distance
                    origin = there * 2 + 1 - side
                    exists = None
                    if distance:
                        exists = there >= 0 if sign < 0 else there < layers
                    arrive(exists, which, cross, origin, group)
                    if cross:
                        forward(exists, which, 1, origin, False, cross_send, to_group, group)

    def pass_rows():
        for j in range(1, shards):
            source = lax.rem(me + shards - j, shards)
            remote(
                x_ref.at[source], xg.at[source, :, columns],
                x_send.at[source], x_recv.at[source], {"seq": source},
            ).wait_recv()

            def share(source=source):
                return remote(
                    xg.at[source, :, columns], xg.at[source, :, columns],
                    t_send.at[source], t_recv.at[source], to_core,
                )

            send(None, share)

    across(0)
    for distance in range(1, layers):
        along(distance)
        across(distance)
        if distance == 1:
            pass_rows()

    others = pl.ds(pl.multiple_of((1 - core) * width, 128), width)
    for j in range(shards):
        source = lax.rem(me + j, shards)
        remote(
            x_ref.at[source], xg.at[source, :, others],
            t_send.at[source], t_recv.at[source], to_core,
        ).wait_recv()
        if j:
            remote(
                d_ref.at[source], dg.at[source], d_send.at[source], d_recv.at[source],
                {"seq": source},
            ).wait_recv()
            for which in range(3):
                arrive(None, which, 1, source, 1 - group)
    for copy in own_copies:
        copy.wait()
    for condition, action in finish:
        when(condition, action)


def exchange(rows, docs, key_weight, value_weight, out_weight):
    shards, groups, tensors = (lax.axis_size(a) for a in ("seq", "groups", "tensor"))
    slot, width = rows.shape[1:]
    dma = pltpu.SemaphoreType.DMA
    any_space = pl.BlockSpec(memory_space=pl.ANY)
    return pl.pallas_call(
        functools.partial(exchange_kernel, shards, groups, tensors),
        out_shape=[
            jax.ShapeDtypeStruct((shards, slot, width * tensors), rows.dtype),
            jax.ShapeDtypeStruct(docs.shape, docs.dtype),
            *(
                jax.ShapeDtypeStruct((shards,) + w.shape, w.dtype)
                for w in (key_weight, value_weight, out_weight)
            ),
        ],
        in_specs=[any_space] * 5,
        out_specs=[any_space] * 5,
        scratch_shapes=[dma((5,))]
        + [dma((shards,))] * 6
        + [dma((6 * shards,))] * 4
        + [dma((9 * shards,))],
        compiler_params=pltpu.CompilerParams(collective_id=0, has_side_effects=True),
    )(rows, docs, key_weight, value_weight, out_weight)


def on_device(enc_rows, enc_owner, enc_doc, dec_doc, queries, key_weight, value_weight, out_weight):
    shard_count = lax.axis_size("seq")
    tensors = lax.axis_size("tensor")
    block_rows = 2 * enc_rows.shape[0] // shard_count
    block_count = enc_rows.shape[0] // block_rows
    slot = -(-block_rows // 16) * 16
    lanes = -(-slot // 128) * 128
    model = enc_rows.shape[1]
    width = model // tensors
    payload = lax.dynamic_slice_in_dim(enc_rows, lax.axis_index("tensor") * width, width, axis=1)
    lead = enc_owner.reshape(block_count, block_rows)[:, 0]
    targets = jnp.arange(shard_count, dtype=jnp.int32)
    blocks = payload.reshape(block_count, block_rows, width)
    blocks = jnp.pad(blocks, ((0, 0), (0, slot - block_rows), (0, 0)))
    doc_blocks = enc_doc.reshape(block_count, block_rows)
    doc_blocks = jnp.pad(doc_blocks, ((0, 0), (0, lanes - block_rows)), constant_values=-1)
    packed = jnp.zeros((shard_count, slot, width), payload.dtype)
    packed_docs = jnp.full((shard_count, lanes), -1, jnp.int32)
    for b in range(block_count):
        chosen = lead[b] == targets
        packed = jnp.where(chosen[:, None, None], blocks[b][None], packed)
        packed_docs = jnp.where(chosen[:, None], doc_blocks[b][None], packed_docs)
    packed_docs = jnp.broadcast_to(packed_docs[:, None, :], (shard_count, 8, lanes))
    arrived, slot_docs, key_full, value_full, out_full = exchange(
        packed, packed_docs, key_weight, value_weight, out_weight
    )
    slots = shard_count * slot
    arrived = arrived.reshape(slots, model)
    slot_docs = slot_docs[:, 0, :slot].reshape(slots)
    inner = key_weight.shape[1]
    keys_here = jnp.dot(
        arrived, key_full.reshape(model, inner), preferred_element_type=jnp.float32
    ).astype(jnp.bfloat16)
    values_here = jnp.dot(
        arrived, value_full.reshape(model, inner), preferred_element_type=jnp.float32
    ).astype(jnp.bfloat16)
    token_count = queries.shape[0]
    head_count = queries.shape[1] // HEAD
    query_heads = queries.reshape(token_count, head_count, HEAD)
    key_heads = keys_here.reshape(slots, head_count, HEAD)
    value_heads = values_here.reshape(slots, head_count, HEAD)
    score_scale = 1.0 / math.sqrt(HEAD)
    scores = (
        jnp.einsum("qhd,khd->hqk", query_heads, key_heads, preferred_element_type=jnp.float32)
        * score_scale
    )
    matching = dec_doc[:, None] == slot_docs[None, :]
    scores = jnp.where(matching[None, :, :], scores, -1e30)
    row_peak = jnp.max(scores, axis=2, keepdims=True)
    exponent = jnp.exp(scores - row_peak)
    probs = (exponent / jnp.sum(exponent, axis=2, keepdims=True)).astype(jnp.bfloat16)
    attended = jnp.einsum("hqk,khd->qhd", probs, value_heads, preferred_element_type=jnp.float32)
    attended = attended.astype(jnp.bfloat16).reshape(token_count, head_count * HEAD)
    partial_rows = jnp.einsum(
        "tk,skn->tsn", attended, out_full, preferred_element_type=jnp.float32
    ).reshape(token_count, shard_count * out_weight.shape[1])
    return lax.psum_scatter(
        partial_rows.astype(jnp.bfloat16), "tensor", scatter_dimension=1, tiled=True
    )


def solution(mesh):
    return jax.shard_map(
        on_device,
        mesh=mesh,
        in_specs=(
            P(("groups", "seq"), None),
            P(("groups", "seq")),
            P(("groups", "seq")),
            P(("groups", "seq")),
            P(("groups", "seq"), "tensor"),
            P("seq", "tensor"),
            P("seq", "tensor"),
            P("tensor", "seq"),
        ),
        out_specs=P(("groups", "seq"), "tensor"),
        check_vma=False,
    )
```

```python
import functools
import math

import jax
import jax.numpy as jnp
from jax import lax
from jax.experimental import pallas as pl
from jax.experimental.pallas import tpu as pltpu
from jax.sharding import PartitionSpec as P

HEAD = 256
MESH = pl.DeviceIdType.MESH


def when(condition, action):
    if condition is None:
        action()
    else:
        pl.when(condition)(action)


def exchange_kernel(
    shards, groups, tensors,
    x_ref, d_ref, k_ref, v_ref, o_ref,
    xg, dg, kg, vg, og,
    local_sem, x_send, x_recv, d_send, d_recv, t_send, t_recv,
    up_send, down_send, side_send, cross_send, recv,
):
    layers = shards // 2
    me = lax.axis_index("seq")
    group = lax.axis_index("groups")
    core = lax.axis_index("tensor")
    layer, side = me // 2, lax.rem(me, 2)
    to_group = {"groups": 1 - group}
    to_core = {"tensor": 1 - core}

    barrier = pltpu.get_barrier_semaphore()
    for j in range(1, shards):
        pl.semaphore_signal(
            barrier, inc=1, device_id={"seq": lax.rem(me + j, shards)}, device_id_type=MESH
        )
    pl.semaphore_signal(barrier, inc=1, device_id=to_group, device_id_type=MESH)
    pl.semaphore_signal(barrier, inc=1, device_id=to_core, device_id_type=MESH)
    pl.semaphore_wait(barrier, shards + 1)

    finish = []
    width = x_ref.shape[2]
    columns = pl.ds(pl.multiple_of(core * width, 128), width)

    def send(condition, make):
        when(condition, lambda: make().start())
        finish.append((condition, lambda: make().wait_send()))

    def remote(src, dst, send_sem, recv_sem, device):
        return pltpu.make_async_remote_copy(
            src_ref=src, dst_ref=dst, send_sem=send_sem, recv_sem=recv_sem,
            device_id=device, device_id_type=MESH,
        )

    weights = ((k_ref, kg, 1), (v_ref, vg, 1), (o_ref, og, 0))

    def piece_of(which, cross, owner):
        ref, axis = weights[which][0], weights[which][2]
        extent = ref.shape[axis]
        plain = extent // 4
        length = (extent - plain) // 2
        if cross:
            cut = pl.ds(pl.multiple_of(plain + owner * length, 128), length)
        else:
            cut = pl.ds(0, plain)
        return (cut, slice(None)) if axis == 0 else (slice(None), cut)

    def forward(condition, which, cross, origin, own, send_sems, device, owner):
        ref, full, _ = weights[which]
        cut = piece_of(which, cross, owner)
        number = (which * 3 + (1 + owner if cross else 0)) * shards + origin
        slot = (which * 2 + cross) * shards + origin

        def make():
            source = ref.at[cut] if own else full.at[(origin,) + cut]
            return remote(
                source, full.at[(origin,) + cut], send_sems.at[slot], recv.at[number], device
            )

        send(condition, make)

    def arrive(condition, which, cross, origin, owner):
        ref, full, _ = weights[which]
        cut = piece_of(which, cross, owner)
        number = (which * 3 + (1 + owner if cross else 0)) * shards + origin

        def wait():
            remote(
                ref.at[cut], full.at[(origin,) + cut],
                cross_send.at[0], recv.at[number], to_group,
            ).wait_recv()

        when(condition, wait)

    def both(a, b):
        return b if a is None else jnp.logical_and(a, b)

    up = {"seq": me + 2}
    down = {"seq": me - 2}
    beside = {"seq": layer * 2 + 1 - side}
    can_up = layer + 1 < layers
    can_down = layer >= 1

    def first(cross):
        for which in range(3):
            forward(None, which, cross, me, True, side_send, beside, group)
            forward(can_up, which, cross, me, True, up_send, up, group)
            forward(can_down, which, cross, me, True, down_send, down, group)

    first(1)

    for j in range(1, shards):
        target = lax.rem(me + j, shards)

        def rows_copy(target=target):
            return remote(
                x_ref.at[target], xg.at[me, :, columns],
                x_send.at[target], x_recv.at[me], {"seq": target},
            )

        def docs_copy(target=target):
            return remote(
                d_ref.at[target], dg.at[me], d_send.at[target], d_recv.at[me], {"seq": target}
            )

        send(None, rows_copy)
        send(None, docs_copy)

    first(0)

    own_copies = [
        pltpu.make_async_copy(x_ref.at[me], xg.at[me, :, columns], local_sem.at[0]),
        pltpu.make_async_copy(d_ref.at[me], dg.at[me], local_sem.at[1]),
        pltpu.make_async_copy(k_ref, kg.at[me], local_sem.at[2]),
        pltpu.make_async_copy(v_ref, vg.at[me], local_sem.at[3]),
        pltpu.make_async_copy(o_ref, og.at[me], local_sem.at[4]),
    ]
    for copy in own_copies:
        copy.start()

    def own_rows():
        return remote(
            x_ref.at[me], xg.at[me, :, columns], t_send.at[me], t_recv.at[me], to_core
        )

    send(None, own_rows)

    def along(distance, cross):
        for which in range(3):
            for sign in (-1, 1):
                there = layer + sign * distance
                origin = there * 2 + side
                exists = there >= 0 if sign < 0 else there < layers
                arrive(exists, which, cross, origin, group)
                if cross:
                    forward(exists, which, 1, origin, False, cross_send, to_group, group)
                if sign < 0:
                    forward(both(exists, can_up), which, cross, origin, False, up_send, up, group)
                else:
                    forward(
                        both(exists, can_down), which, cross, origin, False,
                        down_send, down, group,
                    )
                forward(exists, which, cross, origin, False, side_send, beside, group)

    def across(distance, cross):
        for which in range(3):
            for sign in (-1, 1) if distance else (1,):
                there = layer + sign * distance
                origin = there * 2 + 1 - side
                exists = None
                if distance:
                    exists = there >= 0 if sign < 0 else there < layers
                arrive(exists, which, cross, origin, group)
                if cross:
                    forward(exists, which, 1, origin, False, cross_send, to_group, group)

    def pass_rows():
        for j in range(1, shards):
            source = lax.rem(me + shards - j, shards)
            remote(
                x_ref.at[source], xg.at[source, :, columns],
                x_send.at[source], x_recv.at[source], {"seq": source},
            ).wait_recv()

            def share(source=source):
                return remote(
                    xg.at[source, :, columns], xg.at[source, :, columns],
                    t_send.at[source], t_recv.at[source], to_core,
                )

            send(None, share)

    across(0, 1)
    for distance in range(1, layers):
        along(distance, 1)
        along(distance, 0)
        across(distance, 1)
        if distance == min(2, layers - 1):
            pass_rows()
    for distance in range(layers):
        across(distance, 0)

    others = pl.ds(pl.multiple_of((1 - core) * width, 128), width)
    for j in range(shards):
        source = lax.rem(me + j, shards)
        remote(
            x_ref.at[source], xg.at[source, :, others],
            t_send.at[source], t_recv.at[source], to_core,
        ).wait_recv()
        if j:
            remote(
                d_ref.at[source], dg.at[source], d_send.at[source], d_recv.at[source],
                {"seq": source},
            ).wait_recv()
            for which in range(3):
                arrive(None, which, 1, source, 1 - group)
    for copy in own_copies:
        copy.wait()
    for condition, action in finish:
        when(condition, action)


def exchange(rows, docs, key_weight, value_weight, out_weight):
    shards, groups, tensors = (lax.axis_size(a) for a in ("seq", "groups", "tensor"))
    slot, width = rows.shape[1:]
    dma = pltpu.SemaphoreType.DMA
    any_space = pl.BlockSpec(memory_space=pl.ANY)
    return pl.pallas_call(
        functools.partial(exchange_kernel, shards, groups, tensors),
        out_shape=[
            jax.ShapeDtypeStruct((shards, slot, width * tensors), rows.dtype),
            jax.ShapeDtypeStruct(docs.shape, docs.dtype),
            *(
                jax.ShapeDtypeStruct((shards,) + w.shape, w.dtype)
                for w in (key_weight, value_weight, out_weight)
            ),
        ],
        in_specs=[any_space] * 5,
        out_specs=[any_space] * 5,
        scratch_shapes=[dma((5,))]
        + [dma((shards,))] * 6
        + [dma((6 * shards,))] * 4
        + [dma((9 * shards,))],
        compiler_params=pltpu.CompilerParams(collective_id=0, has_side_effects=True),
    )(rows, docs, key_weight, value_weight, out_weight)


def on_device(enc_rows, enc_owner, enc_doc, dec_doc, queries, key_weight, value_weight, out_weight):
    shard_count = lax.axis_size("seq")
    tensors = lax.axis_size("tensor")
    block_rows = 2 * enc_rows.shape[0] // shard_count
    block_count = enc_rows.shape[0] // block_rows
    slot = -(-block_rows // 16) * 16
    lanes = -(-slot // 128) * 128
    model = enc_rows.shape[1]
    width = model // tensors
    payload = lax.dynamic_slice_in_dim(enc_rows, lax.axis_index("tensor") * width, width, axis=1)
    lead = enc_owner.reshape(block_count, block_rows)[:, 0]
    targets = jnp.arange(shard_count, dtype=jnp.int32)
    blocks = payload.reshape(block_count, block_rows, width)
    blocks = jnp.pad(blocks, ((0, 0), (0, slot - block_rows), (0, 0)))
    doc_blocks = enc_doc.reshape(block_count, block_rows)
    doc_blocks = jnp.pad(doc_blocks, ((0, 0), (0, lanes - block_rows)), constant_values=-1)
    packed = jnp.zeros((shard_count, slot, width), payload.dtype)
    packed_docs = jnp.full((shard_count, lanes), -1, jnp.int32)
    for b in range(block_count):
        chosen = lead[b] == targets
        packed = jnp.where(chosen[:, None, None], blocks[b][None], packed)
        packed_docs = jnp.where(chosen[:, None], doc_blocks[b][None], packed_docs)
    packed_docs = jnp.broadcast_to(packed_docs[:, None, :], (shard_count, 8, lanes))
    arrived, slot_docs, key_full, value_full, out_full = exchange(
        packed, packed_docs, key_weight, value_weight, out_weight
    )
    slots = shard_count * slot
    arrived = arrived.reshape(slots, model)
    slot_docs = slot_docs[:, 0, :slot].reshape(slots)
    inner = key_weight.shape[1]
    keys_here = jnp.dot(
        arrived, key_full.reshape(model, inner), preferred_element_type=jnp.float32
    ).astype(jnp.bfloat16)
    values_here = jnp.dot(
        arrived, value_full.reshape(model, inner), preferred_element_type=jnp.float32
    ).astype(jnp.bfloat16)
    token_count = queries.shape[0]
    head_count = queries.shape[1] // HEAD
    query_heads = queries.reshape(token_count, head_count, HEAD)
    key_heads = keys_here.reshape(slots, head_count, HEAD)
    value_heads = values_here.reshape(slots, head_count, HEAD)
    score_scale = 1.0 / math.sqrt(HEAD)
    scores = (
        jnp.einsum("qhd,khd->hqk", query_heads, key_heads, preferred_element_type=jnp.float32)
        * score_scale
    )
    matching = dec_doc[:, None] == slot_docs[None, :]
    scores = jnp.where(matching[None, :, :], scores, -1e30)
    row_peak = jnp.max(scores, axis=2, keepdims=True)
    exponent = jnp.exp(scores - row_peak)
    probs = (exponent / jnp.sum(exponent, axis=2, keepdims=True)).astype(jnp.bfloat16)
    attended = jnp.einsum("hqk,khd->qhd", probs, value_heads, preferred_element_type=jnp.float32)
    attended = attended.astype(jnp.bfloat16).reshape(token_count, head_count * HEAD)
    partial_rows = jnp.concatenate(
        [
            jnp.dot(attended, out_full[s], preferred_element_type=jnp.float32).astype(jnp.bfloat16)
            for s in range(shard_count)
        ],
        axis=1,
    )
    return lax.psum_scatter(
        partial_rows, "tensor", scatter_dimension=1, tiled=True
    )


def solution(mesh):
    return jax.shard_map(
        on_device,
        mesh=mesh,
        in_specs=(
            P(("groups", "seq"), None),
            P(("groups", "seq")),
            P(("groups", "seq")),
            P(("groups", "seq")),
            P(("groups", "seq"), "tensor"),
            P("seq", "tensor"),
            P("seq", "tensor"),
            P("tensor", "seq"),
        ),
        out_specs=P(("groups", "seq"), "tensor"),
        check_vma=False,
    )
```

```python
import functools
import math

import jax
import jax.numpy as jnp
from jax import lax
from jax.experimental import pallas as pl
from jax.experimental.pallas import tpu as pltpu
from jax.sharding import PartitionSpec as P

HEAD = 256
MESH = pl.DeviceIdType.MESH


def when(condition, action):
    if condition is None:
        action()
    else:
        pl.when(condition)(action)


def exchange_kernel(
    shards, groups, tensors,
    x_ref, d_ref, k_ref, v_ref, o_ref,
    xg, dg, kg, vg, og,
    local_sem, x_send, x_recv, d_send, d_recv, t_send, t_recv,
    up_send, down_send, side_send, cross_send, recv,
):
    layers = shards // 2
    me = lax.axis_index("seq")
    group = lax.axis_index("groups")
    core = lax.axis_index("tensor")
    layer, side = me // 2, lax.rem(me, 2)
    to_group = {"groups": 1 - group}
    to_core = {"tensor": 1 - core}

    barrier = pltpu.get_barrier_semaphore()
    for j in range(1, shards):
        pl.semaphore_signal(
            barrier, inc=1, device_id={"seq": lax.rem(me + j, shards)}, device_id_type=MESH
        )
    pl.semaphore_signal(barrier, inc=1, device_id=to_group, device_id_type=MESH)
    pl.semaphore_signal(barrier, inc=1, device_id=to_core, device_id_type=MESH)
    pl.semaphore_wait(barrier, shards + 1)

    finish = []
    width = x_ref.shape[2]
    columns = pl.ds(pl.multiple_of(core * width, 128), width)

    def send(condition, make):
        when(condition, lambda: make().start())
        finish.append((condition, lambda: make().wait_send()))

    def remote(src, dst, send_sem, recv_sem, device):
        return pltpu.make_async_remote_copy(
            src_ref=src, dst_ref=dst, send_sem=send_sem, recv_sem=recv_sem,
            device_id=device, device_id_type=MESH,
        )

    weights = ((k_ref, kg, 1), (v_ref, vg, 1), (o_ref, og, 0))

    def piece_of(which, cross, owner):
        ref, axis = weights[which][0], weights[which][2]
        extent = ref.shape[axis]
        plain = extent // 4
        length = (extent - plain) // 2
        if cross:
            cut = pl.ds(pl.multiple_of(plain + owner * length, 128), length)
        else:
            cut = pl.ds(0, plain)
        return (cut, slice(None)) if axis == 0 else (slice(None), cut)

    def forward(condition, which, cross, origin, own, send_sems, device, owner):
        ref, full, _ = weights[which]
        cut = piece_of(which, cross, owner)
        number = (which * 3 + (1 + owner if cross else 0)) * shards + origin
        slot = (which * 2 + cross) * shards + origin

        def make():
            source = ref.at[cut] if own else full.at[(origin,) + cut]
            return remote(
                source, full.at[(origin,) + cut], send_sems.at[slot], recv.at[number], device
            )

        send(condition, make)

    def arrive(condition, which, cross, origin, owner):
        ref, full, _ = weights[which]
        cut = piece_of(which, cross, owner)
        number = (which * 3 + (1 + owner if cross else 0)) * shards + origin

        def wait():
            remote(
                ref.at[cut], full.at[(origin,) + cut],
                cross_send.at[0], recv.at[number], to_group,
            ).wait_recv()

        when(condition, wait)

    def both(a, b):
        return b if a is None else jnp.logical_and(a, b)

    up = {"seq": me + 2}
    down = {"seq": me - 2}
    beside = {"seq": layer * 2 + 1 - side}
    can_up = layer + 1 < layers
    can_down = layer >= 1

    def first(cross):
        for which in range(3):
            forward(None, which, cross, me, True, side_send, beside, group)
            forward(can_up, which, cross, me, True, up_send, up, group)
            forward(can_down, which, cross, me, True, down_send, down, group)

    first(1)

    for j in range(1, shards):
        target = lax.rem(me + j, shards)

        def rows_copy(target=target):
            return remote(
                x_ref.at[target], xg.at[me, :, columns],
                x_send.at[target], x_recv.at[me], {"seq": target},
            )

        def docs_copy(target=target):
            return remote(
                d_ref.at[target], dg.at[me], d_send.at[target], d_recv.at[me], {"seq": target}
            )

        send(None, rows_copy)
        send(None, docs_copy)

    first(0)

    own_copies = [
        pltpu.make_async_copy(x_ref.at[me], xg.at[me, :, columns], local_sem.at[0]),
        pltpu.make_async_copy(d_ref.at[me], dg.at[me], local_sem.at[1]),
        pltpu.make_async_copy(k_ref, kg.at[me], local_sem.at[2]),
        pltpu.make_async_copy(v_ref, vg.at[me], local_sem.at[3]),
        pltpu.make_async_copy(o_ref, og.at[me], local_sem.at[4]),
    ]
    for copy in own_copies:
        copy.start()

    def own_rows():
        return remote(
            x_ref.at[me], xg.at[me, :, columns], t_send.at[me], t_recv.at[me], to_core
        )

    send(None, own_rows)

    def along(distance, cross):
        for which in range(3):
            for sign in (-1, 1):
                there = layer + sign * distance
                origin = there * 2 + side
                exists = there >= 0 if sign < 0 else there < layers
                arrive(exists, which, cross, origin, group)
                if cross:
                    forward(exists, which, 1, origin, False, cross_send, to_group, group)
                if sign < 0:
                    forward(both(exists, can_up), which, cross, origin, False, up_send, up, group)
                else:
                    forward(
                        both(exists, can_down), which, cross, origin, False,
                        down_send, down, group,
                    )
                forward(exists, which, cross, origin, False, side_send, beside, group)

    def across(distance, cross):
        for which in range(3):
            for sign in (-1, 1) if distance else (1,):
                there = layer + sign * distance
                origin = there * 2 + 1 - side
                exists = None
                if distance:
                    exists = there >= 0 if sign < 0 else there < layers
                arrive(exists, which, cross, origin, group)
                if cross:
                    forward(exists, which, 1, origin, False, cross_send, to_group, group)

    def pass_rows():
        for j in range(1, shards):
            source = lax.rem(me + shards - j, shards)
            remote(
                x_ref.at[source], xg.at[source, :, columns],
                x_send.at[source], x_recv.at[source], {"seq": source},
            ).wait_recv()

            def share(source=source):
                return remote(
                    xg.at[source, :, columns], xg.at[source, :, columns],
                    t_send.at[source], t_recv.at[source], to_core,
                )

            send(None, share)

    across(0, 1)
    for distance in range(1, layers):
        along(distance, 1)
        along(distance, 0)
        across(distance, 1)
        if distance == min(2, layers - 1):
            pass_rows()
    for distance in range(layers):
        across(distance, 0)

    others = pl.ds(pl.multiple_of((1 - core) * width, 128), width)
    for j in range(shards):
        source = lax.rem(me + j, shards)
        remote(
            x_ref.at[source], xg.at[source, :, others],
            t_send.at[source], t_recv.at[source], to_core,
        ).wait_recv()
        if j:
            remote(
                d_ref.at[source], dg.at[source], d_send.at[source], d_recv.at[source],
                {"seq": source},
            ).wait_recv()
            for which in range(3):
                arrive(None, which, 1, source, 1 - group)
    for copy in own_copies:
        copy.wait()
    for condition, action in finish:
        when(condition, action)


def exchange(rows, docs, key_weight, value_weight, out_weight):
    shards, groups, tensors = (lax.axis_size(a) for a in ("seq", "groups", "tensor"))
    slot, width = rows.shape[1:]
    dma = pltpu.SemaphoreType.DMA
    any_space = pl.BlockSpec(memory_space=pl.ANY)
    return pl.pallas_call(
        functools.partial(exchange_kernel, shards, groups, tensors),
        out_shape=[
            jax.ShapeDtypeStruct((shards, slot, width * tensors), rows.dtype),
            jax.ShapeDtypeStruct(docs.shape, docs.dtype),
            *(
                jax.ShapeDtypeStruct((shards,) + w.shape, w.dtype)
                for w in (key_weight, value_weight, out_weight)
            ),
        ],
        in_specs=[any_space] * 5,
        out_specs=[any_space] * 5,
        scratch_shapes=[dma((5,))]
        + [dma((shards,))] * 6
        + [dma((6 * shards,))] * 4
        + [dma((9 * shards,))],
        compiler_params=pltpu.CompilerParams(collective_id=0, has_side_effects=True),
    )(rows, docs, key_weight, value_weight, out_weight)


def attend_kernel(
    steps, x_ref, k_ref, v_ref, q_ref, dec_ref, docs_ref, o_ref, out_ref,
    key_sums, value_sums, attended,
):
    step = pl.program_id(0)

    @pl.when(step == 0)
    def _():
        key_sums[...] = jnp.zeros_like(key_sums)
        value_sums[...] = jnp.zeros_like(value_sums)

    @pl.when(step < steps)
    def _():
        rows = x_ref[...]
        key_sums[...] += jnp.dot(rows, k_ref[...], preferred_element_type=jnp.float32)
        value_sums[...] += jnp.dot(rows, v_ref[...], preferred_element_type=jnp.float32)

    @pl.when(step == steps - 1)
    def _():
        matching = dec_ref[...] == docs_ref[...]
        for head in range(q_ref.shape[1] // HEAD):
            cut = slice(head * HEAD, (head + 1) * HEAD)
            scores = lax.dot_general(
                q_ref[:, cut], key_sums[:, cut].astype(jnp.bfloat16),
                (((1,), (1,)), ((), ())), preferred_element_type=jnp.float32,
            )
            scores = jnp.where(matching, scores * (1.0 / math.sqrt(HEAD)), -1e30)
            exponent = jnp.exp(scores - jnp.max(scores, axis=1, keepdims=True))
            probs = (exponent / jnp.sum(exponent, axis=1, keepdims=True)).astype(jnp.bfloat16)
            attended[:, cut] = jnp.dot(
                probs, value_sums[:, cut].astype(jnp.bfloat16),
                preferred_element_type=jnp.float32,
            ).astype(jnp.bfloat16)

    @pl.when(step >= steps)
    def _():
        width = o_ref.shape[2]
        for shard in range(o_ref.shape[0]):
            out_ref[:, shard * width : (shard + 1) * width] = jnp.dot(
                attended[...], o_ref[shard], preferred_element_type=jnp.float32
            ).astype(jnp.bfloat16)


def attend(rows, key_full, value_full, queries, dec_doc, slot_docs, out_full):
    slots, model = rows.shape
    inner = key_full.shape[1]
    tokens = queries.shape[0]
    shards, _, width = out_full.shape
    block = 512
    steps = model // block
    per_block = block // width

    def project_step(i):
        return jnp.minimum(i, steps - 1)

    def output_step(i):
        return jnp.maximum(i - steps, 0)

    def whole(shape):
        return pl.BlockSpec(shape, lambda i: (0, 0))

    return pl.pallas_call(
        functools.partial(attend_kernel, steps),
        grid=(steps + shards // per_block,),
        out_shape=jax.ShapeDtypeStruct((tokens, shards * width), jnp.bfloat16),
        in_specs=[
            pl.BlockSpec((slots, block), lambda i: (0, project_step(i))),
            pl.BlockSpec((block, inner), lambda i: (project_step(i), 0)),
            pl.BlockSpec((block, inner), lambda i: (project_step(i), 0)),
            whole(queries.shape),
            whole(dec_doc.shape),
            whole(slot_docs.shape),
            pl.BlockSpec((per_block, inner, width), lambda i: (output_step(i), 0, 0)),
        ],
        out_specs=pl.BlockSpec((tokens, block), lambda i: (0, output_step(i))),
        scratch_shapes=[
            pltpu.VMEM((slots, inner), jnp.float32),
            pltpu.VMEM((slots, inner), jnp.float32),
            pltpu.VMEM((tokens, inner), jnp.bfloat16),
        ],
        compiler_params=pltpu.CompilerParams(vmem_limit_bytes=40 * 1024 * 1024),
    )(rows, key_full, value_full, queries, dec_doc, slot_docs, out_full)


def on_device(enc_rows, enc_owner, enc_doc, dec_doc, queries, key_weight, value_weight, out_weight):
    shard_count = lax.axis_size("seq")
    tensors = lax.axis_size("tensor")
    block_rows = 2 * enc_rows.shape[0] // shard_count
    block_count = enc_rows.shape[0] // block_rows
    slot = -(-block_rows // 16) * 16
    lanes = -(-slot // 128) * 128
    model = enc_rows.shape[1]
    width = model // tensors
    payload = lax.dynamic_slice_in_dim(enc_rows, lax.axis_index("tensor") * width, width, axis=1)
    lead = enc_owner.reshape(block_count, block_rows)[:, 0]
    targets = jnp.arange(shard_count, dtype=jnp.int32)
    blocks = payload.reshape(block_count, block_rows, width)
    blocks = jnp.pad(blocks, ((0, 0), (0, slot - block_rows), (0, 0)))
    doc_blocks = enc_doc.reshape(block_count, block_rows)
    doc_blocks = jnp.pad(doc_blocks, ((0, 0), (0, lanes - block_rows)), constant_values=-1)
    packed = jnp.zeros((shard_count, slot, width), payload.dtype)
    packed_docs = jnp.full((shard_count, lanes), -1, jnp.int32)
    for b in range(block_count):
        chosen = lead[b] == targets
        packed = jnp.where(chosen[:, None, None], blocks[b][None], packed)
        packed_docs = jnp.where(chosen[:, None], doc_blocks[b][None], packed_docs)
    packed_docs = jnp.broadcast_to(packed_docs[:, None, :], (shard_count, 8, lanes))
    arrived, slot_docs, key_full, value_full, out_full = exchange(
        packed, packed_docs, key_weight, value_weight, out_weight
    )
    slots = shard_count * slot
    partial_rows = attend(
        arrived.reshape(slots, model),
        key_full.reshape(model, key_weight.shape[1]),
        value_full.reshape(model, value_weight.shape[1]),
        queries,
        dec_doc[:, None],
        slot_docs[:, 0, :slot].reshape(1, slots),
        out_full,
    )
    return lax.psum_scatter(
        partial_rows, "tensor", scatter_dimension=1, tiled=True
    )


def solution(mesh):
    return jax.shard_map(
        on_device,
        mesh=mesh,
        in_specs=(
            P(("groups", "seq"), None),
            P(("groups", "seq")),
            P(("groups", "seq")),
            P(("groups", "seq")),
            P(("groups", "seq"), "tensor"),
            P("seq", "tensor"),
            P("seq", "tensor"),
            P("tensor", "seq"),
        ),
        out_specs=P(("groups", "seq"), "tensor"),
        check_vma=False,
    )
```

```python
import functools
import math

import jax
import jax.numpy as jnp
from jax import lax
from jax.experimental import pallas as pl
from jax.experimental.pallas import tpu as pltpu
from jax.sharding import PartitionSpec as P

HEAD = 256
MESH = pl.DeviceIdType.MESH


def when(condition, action):
    if condition is None:
        action()
    else:
        pl.when(condition)(action)


def exchange_kernel(
    shards, groups, tensors,
    x_ref, d_ref, k_ref, v_ref, o_ref,
    xg, dg, kg, vg, og,
    local_sem, x_send, x_recv, d_send, d_recv, t_send, t_recv,
    up_send, down_send, side_send, cross_send, recv,
):
    layers = shards // 2
    me = lax.axis_index("seq")
    group = lax.axis_index("groups")
    core = lax.axis_index("tensor")
    layer, side = me // 2, lax.rem(me, 2)
    to_group = {"groups": 1 - group}
    to_core = {"tensor": 1 - core}

    barrier = pltpu.get_barrier_semaphore()
    for j in range(1, shards):
        pl.semaphore_signal(
            barrier, inc=1, device_id={"seq": lax.rem(me + j, shards)}, device_id_type=MESH
        )
    pl.semaphore_signal(barrier, inc=1, device_id=to_group, device_id_type=MESH)
    pl.semaphore_signal(barrier, inc=1, device_id=to_core, device_id_type=MESH)
    pl.semaphore_wait(barrier, shards + 1)

    finish = []
    width = x_ref.shape[2]
    columns = pl.ds(pl.multiple_of(core * width, 128), width)

    def send(condition, make):
        when(condition, lambda: make().start())
        finish.append((condition, lambda: make().wait_send()))

    def remote(src, dst, send_sem, recv_sem, device):
        return pltpu.make_async_remote_copy(
            src_ref=src, dst_ref=dst, send_sem=send_sem, recv_sem=recv_sem,
            device_id=device, device_id_type=MESH,
        )

    weights = ((k_ref, kg, 1), (v_ref, vg, 1), (o_ref, og, 0))

    def piece_of(which, cross, owner):
        ref, axis = weights[which][0], weights[which][2]
        extent = ref.shape[axis]
        plain = extent // 4
        length = (extent - plain) // 2
        if cross:
            cut = pl.ds(pl.multiple_of(plain + owner * length, 128), length)
        else:
            cut = pl.ds(0, plain)
        return (cut, slice(None)) if axis == 0 else (slice(None), cut)

    def forward(condition, which, cross, origin, own, send_sems, device, owner):
        ref, full, _ = weights[which]
        cut = piece_of(which, cross, owner)
        number = (which * 3 + (1 + owner if cross else 0)) * shards + origin
        slot = (which * 2 + cross) * shards + origin

        def make():
            source = ref.at[cut] if own else full.at[(origin,) + cut]
            return remote(
                source, full.at[(origin,) + cut], send_sems.at[slot], recv.at[number], device
            )

        send(condition, make)

    def arrive(condition, which, cross, origin, owner):
        ref, full, _ = weights[which]
        cut = piece_of(which, cross, owner)
        number = (which * 3 + (1 + owner if cross else 0)) * shards + origin

        def wait():
            remote(
                ref.at[cut], full.at[(origin,) + cut],
                cross_send.at[0], recv.at[number], to_group,
            ).wait_recv()

        when(condition, wait)

    def both(a, b):
        return b if a is None else jnp.logical_and(a, b)

    up = {"seq": me + 2}
    down = {"seq": me - 2}
    beside = {"seq": layer * 2 + 1 - side}
    can_up = layer + 1 < layers
    can_down = layer >= 1

    def first(cross):
        for which in range(3):
            forward(None, which, cross, me, True, side_send, beside, group)
            forward(can_up, which, cross, me, True, up_send, up, group)
            forward(can_down, which, cross, me, True, down_send, down, group)

    first(1)

    first(0)

    own_copies = [
        pltpu.make_async_copy(x_ref.at[me], xg.at[me, :, columns], local_sem.at[0]),
        pltpu.make_async_copy(d_ref.at[me], dg.at[me], local_sem.at[1]),
        pltpu.make_async_copy(k_ref, kg.at[me], local_sem.at[2]),
        pltpu.make_async_copy(v_ref, vg.at[me], local_sem.at[3]),
        pltpu.make_async_copy(o_ref, og.at[me], local_sem.at[4]),
    ]
    for copy in own_copies:
        copy.start()

    def own_rows():
        return remote(
            x_ref.at[me], xg.at[me, :, columns], t_send.at[me], t_recv.at[me], to_core
        )

    send(None, own_rows)

    def along(distance, cross):
        for which in range(3):
            for sign in (-1, 1):
                there = layer + sign * distance
                origin = there * 2 + side
                exists = there >= 0 if sign < 0 else there < layers
                arrive(exists, which, cross, origin, group)
                if cross:
                    forward(exists, which, 1, origin, False, cross_send, to_group, group)
                if sign < 0:
                    forward(both(exists, can_up), which, cross, origin, False, up_send, up, group)
                else:
                    forward(
                        both(exists, can_down), which, cross, origin, False,
                        down_send, down, group,
                    )
                forward(exists, which, cross, origin, False, side_send, beside, group)

    def across(distance, cross):
        for which in range(3):
            for sign in (-1, 1) if distance else (1,):
                there = layer + sign * distance
                origin = there * 2 + 1 - side
                exists = None
                if distance:
                    exists = there >= 0 if sign < 0 else there < layers
                arrive(exists, which, cross, origin, group)
                if cross:
                    forward(exists, which, 1, origin, False, cross_send, to_group, group)

    def send_rows():
        for j in range(1, shards):
            target = lax.rem(me + j, shards)

            def rows_copy(target=target):
                return remote(
                    x_ref.at[target], xg.at[me, :, columns],
                    x_send.at[target], x_recv.at[me], {"seq": target},
                )

            def docs_copy(target=target):
                return remote(
                    d_ref.at[target], dg.at[me], d_send.at[target], d_recv.at[me], {"seq": target}
                )

            send(None, rows_copy)
            send(None, docs_copy)

    def pass_rows():
        for j in range(1, shards):
            source = lax.rem(me + shards - j, shards)
            remote(
                x_ref.at[source], xg.at[source, :, columns],
                x_send.at[source], x_recv.at[source], {"seq": source},
            ).wait_recv()

            def share(source=source):
                return remote(
                    xg.at[source, :, columns], xg.at[source, :, columns],
                    t_send.at[source], t_recv.at[source], to_core,
                )

            send(None, share)

    across(0, 1)
    for distance in range(1, layers):
        along(distance, 1)
        along(distance, 0)
        across(distance, 1)
        if distance == 1:
            send_rows()
    pass_rows()
    for distance in range(layers):
        across(distance, 0)

    others = pl.ds(pl.multiple_of((1 - core) * width, 128), width)
    for j in range(shards):
        source = lax.rem(me + j, shards)
        remote(
            x_ref.at[source], xg.at[source, :, others],
            t_send.at[source], t_recv.at[source], to_core,
        ).wait_recv()
        if j:
            remote(
                d_ref.at[source], dg.at[source], d_send.at[source], d_recv.at[source],
                {"seq": source},
            ).wait_recv()
            for which in range(3):
                arrive(None, which, 1, source, 1 - group)
    for copy in own_copies:
        copy.wait()
    for condition, action in finish:
        when(condition, action)


def exchange(rows, docs, key_weight, value_weight, out_weight):
    shards, groups, tensors = (lax.axis_size(a) for a in ("seq", "groups", "tensor"))
    slot, width = rows.shape[1:]
    dma = pltpu.SemaphoreType.DMA
    any_space = pl.BlockSpec(memory_space=pl.ANY)
    return pl.pallas_call(
        functools.partial(exchange_kernel, shards, groups, tensors),
        out_shape=[
            jax.ShapeDtypeStruct((shards, slot, width * tensors), rows.dtype),
            jax.ShapeDtypeStruct(docs.shape, docs.dtype),
            *(
                jax.ShapeDtypeStruct((shards,) + w.shape, w.dtype)
                for w in (key_weight, value_weight, out_weight)
            ),
        ],
        in_specs=[any_space] * 5,
        out_specs=[any_space] * 5,
        scratch_shapes=[dma((5,))]
        + [dma((shards,))] * 6
        + [dma((6 * shards,))] * 4
        + [dma((9 * shards,))],
        compiler_params=pltpu.CompilerParams(collective_id=0, has_side_effects=True),
    )(rows, docs, key_weight, value_weight, out_weight)


def attend_kernel(
    steps, x_ref, k_ref, v_ref, q_ref, dec_ref, docs_ref, o_ref, out_ref,
    key_sums, value_sums, attended,
):
    step = pl.program_id(0)

    @pl.when(step == 0)
    def _():
        key_sums[...] = jnp.zeros_like(key_sums)
        value_sums[...] = jnp.zeros_like(value_sums)

    @pl.when(step < steps)
    def _():
        rows = x_ref[...]
        key_sums[...] += jnp.dot(rows, k_ref[...], preferred_element_type=jnp.float32)
        value_sums[...] += jnp.dot(rows, v_ref[...], preferred_element_type=jnp.float32)

    @pl.when(step == steps - 1)
    def _():
        matching = dec_ref[...] == docs_ref[...]
        for head in range(q_ref.shape[1] // HEAD):
            cut = slice(head * HEAD, (head + 1) * HEAD)
            scores = lax.dot_general(
                q_ref[:, cut], key_sums[:, cut].astype(jnp.bfloat16),
                (((1,), (1,)), ((), ())), preferred_element_type=jnp.float32,
            )
            scores = jnp.where(matching, scores * (1.0 / math.sqrt(HEAD)), -1e30)
            exponent = jnp.exp(scores - jnp.max(scores, axis=1, keepdims=True))
            probs = (exponent / jnp.sum(exponent, axis=1, keepdims=True)).astype(jnp.bfloat16)
            attended[:, cut] = jnp.dot(
                probs, value_sums[:, cut].astype(jnp.bfloat16),
                preferred_element_type=jnp.float32,
            ).astype(jnp.bfloat16)

    @pl.when(step >= steps)
    def _():
        width = o_ref.shape[2]
        for shard in range(o_ref.shape[0]):
            out_ref[:, shard * width : (shard + 1) * width] = jnp.dot(
                attended[...], o_ref[shard], preferred_element_type=jnp.float32
            ).astype(jnp.bfloat16)


def attend(rows, key_full, value_full, queries, dec_doc, slot_docs, out_full):
    slots, model = rows.shape
    inner = key_full.shape[1]
    tokens = queries.shape[0]
    shards, _, width = out_full.shape
    block = 512
    steps = model // block
    per_block = block // width

    def project_step(i):
        return jnp.minimum(i, steps - 1)

    def output_step(i):
        return jnp.maximum(i - steps, 0)

    def whole(shape):
        return pl.BlockSpec(shape, lambda i: (0, 0))

    return pl.pallas_call(
        functools.partial(attend_kernel, steps),
        grid=(steps + shards // per_block,),
        out_shape=jax.ShapeDtypeStruct((tokens, shards * width), jnp.bfloat16),
        in_specs=[
            pl.BlockSpec((slots, block), lambda i: (0, project_step(i))),
            pl.BlockSpec((block, inner), lambda i: (project_step(i), 0)),
            pl.BlockSpec((block, inner), lambda i: (project_step(i), 0)),
            whole(queries.shape),
            whole(dec_doc.shape),
            whole(slot_docs.shape),
            pl.BlockSpec((per_block, inner, width), lambda i: (output_step(i), 0, 0)),
        ],
        out_specs=pl.BlockSpec((tokens, block), lambda i: (0, output_step(i))),
        scratch_shapes=[
            pltpu.VMEM((slots, inner), jnp.float32),
            pltpu.VMEM((slots, inner), jnp.float32),
            pltpu.VMEM((tokens, inner), jnp.bfloat16),
        ],
        compiler_params=pltpu.CompilerParams(vmem_limit_bytes=40 * 1024 * 1024),
    )(rows, key_full, value_full, queries, dec_doc, slot_docs, out_full)


def on_device(enc_rows, enc_owner, enc_doc, dec_doc, queries, key_weight, value_weight, out_weight):
    shard_count = lax.axis_size("seq")
    tensors = lax.axis_size("tensor")
    block_rows = 2 * enc_rows.shape[0] // shard_count
    block_count = enc_rows.shape[0] // block_rows
    slot = -(-block_rows // 16) * 16
    lanes = -(-slot // 128) * 128
    model = enc_rows.shape[1]
    width = model // tensors
    payload = lax.dynamic_slice_in_dim(enc_rows, lax.axis_index("tensor") * width, width, axis=1)
    lead = enc_owner.reshape(block_count, block_rows)[:, 0]
    targets = jnp.arange(shard_count, dtype=jnp.int32)
    blocks = payload.reshape(block_count, block_rows, width)
    blocks = jnp.pad(blocks, ((0, 0), (0, slot - block_rows), (0, 0)))
    doc_blocks = enc_doc.reshape(block_count, block_rows)
    doc_blocks = jnp.pad(doc_blocks, ((0, 0), (0, lanes - block_rows)), constant_values=-1)
    packed = jnp.zeros((shard_count, slot, width), payload.dtype)
    packed_docs = jnp.full((shard_count, lanes), -1, jnp.int32)
    for b in range(block_count):
        chosen = lead[b] == targets
        packed = jnp.where(chosen[:, None, None], blocks[b][None], packed)
        packed_docs = jnp.where(chosen[:, None], doc_blocks[b][None], packed_docs)
    packed_docs = jnp.broadcast_to(packed_docs[:, None, :], (shard_count, 8, lanes))
    arrived, slot_docs, key_full, value_full, out_full = exchange(
        packed, packed_docs, key_weight, value_weight, out_weight
    )
    slots = shard_count * slot
    partial_rows = attend(
        arrived.reshape(slots, model),
        key_full.reshape(model, key_weight.shape[1]),
        value_full.reshape(model, value_weight.shape[1]),
        queries,
        dec_doc[:, None],
        slot_docs[:, 0, :slot].reshape(1, slots),
        out_full,
    )
    return lax.psum_scatter(
        partial_rows, "tensor", scatter_dimension=1, tiled=True
    )


def solution(mesh):
    return jax.shard_map(
        on_device,
        mesh=mesh,
        in_specs=(
            P(("groups", "seq"), None),
            P(("groups", "seq")),
            P(("groups", "seq")),
            P(("groups", "seq")),
            P(("groups", "seq"), "tensor"),
            P("seq", "tensor"),
            P("seq", "tensor"),
            P("tensor", "seq"),
        ),
        out_specs=P(("groups", "seq"), "tensor"),
        check_vma=False,
    )
```
